32 devices in a mesh: batch: 2 (over x), height: 4 (over y, core), width: 4 (over z).
Axes of the slice: x: 2, y: 2, z: 4, core: 2. Of those that a mesh axis runs over, the one named last changes fastest.
Arguments:
- image_query: bfloat16 [128, 32, 3072], P(('batch', 'height'), 'width'), parts along dimension 0, may hold values from -60 to 60
- image_key: bfloat16 [128, 32, 3072], P(('batch', 'height'), 'width'), parts along dimension 0, may hold values from -6 to 6
- image_value: bfloat16 [128, 32, 3072], P(('batch', 'height'), 'width'), parts along dimension 0, may hold values from -6 to 6
- text_query: bfloat16 [512, 3072], P(('batch', 'width')), parts along dimension 0, may hold values from -60 to 60
- text_key: bfloat16 [512, 3072], P(('batch', 'width')), parts along dimension 0, may hold values from -6 to 6
- text_value: bfloat16 [512, 3072], P(('batch', 'width')), parts along dimension 0, may hold values from -6 to 6
- text_length: int32 [2], P('batch'), parts along dimension 0, may hold values from 64 to 256
Outputs:
- image_out: bfloat16 [128, 32, 3072], P(('batch', 'height'), 'width'), parts along dimension 0
- text_out: bfloat16 [512, 3072], P(('batch', 'width')), parts along dimension 0
The draws below stay inside these ranges and needn't reach their ends.
There are 2 independent parts, one for each index of `batch`. The reference program is written for one: setup_inputs(seed, part) draws one part's arguments, and reference() takes and returns one part's arrays. A program takes and returns all parts, laid end to end along the dimension named above; each array names one. Nothing has to cross between parts.
All inputs are finite; a program needn't handle non-finite values.
Results may differ from the reference program's by a relative error of at most 0.0034.
Values may be sent and summed in bfloat16 or wider, within the bound.
A program may use at most 128 MiB of HBM per device.

```python
import jax
import jax.numpy as jnp
from jax import lax

HEADS = 24
HEAD_DIM = 128
D = 3072
TH = 16
TW = 8
RADIUS = 8
TXT = 256
HT = 64
WT = 32
N_HEIGHT = 4
N_WIDTH = 4


def shared_keys(key):
    image_part = jnp.clip(jax.random.normal(jax.random.fold_in(key, 101), (HT, WT, D), jnp.float32), -6.0, 6.0)
    text_part = jnp.clip(jax.random.normal(jax.random.fold_in(key, 102), (TXT, D), jnp.float32), -6.0, 6.0)
    return (image_part, text_part)


def draw_image_key(key, part):
    return shared_keys(key)[0].astype(jnp.bfloat16)


def draw_text_key(key, part):
    return shared_keys(key)[1].astype(jnp.bfloat16)


def draw_image_query(key, part):
    return (2.5 * jnp.clip(jax.random.normal(jax.random.fold_in(key, 103), (HT, WT, D), jnp.float32), -6.0, 6.0)).astype(jnp.bfloat16)


def draw_text_query(key, part):
    return (3.5 * jnp.clip(jax.random.normal(jax.random.fold_in(key, 106), (TXT, D), jnp.float32), -6.0, 6.0)).astype(jnp.bfloat16)


def block_levels(rng, extent, split, smallest, largest):
    factor_of = 1.0
    for axis_at, shards_of in split:
        draws = jax.random.uniform(jax.random.fold_in(jax.random.fold_in(rng, 6), axis_at), (shards_of,), jnp.float32, smallest / len(split), largest / len(split))
        factor_of = factor_of * jnp.repeat(jnp.exp(draws), extent[axis_at] // shards_of).reshape((-1,) + (1,) * (len(extent) - 1 - axis_at))
    return factor_of


def noise(key, extent, scale, bound, cuts=(), kind=jnp.bfloat16):
    values = jax.random.normal(key, extent, jnp.float32) * scale
    if len(cuts) > 0:
        values = block_levels(key, extent, cuts, -0.22, 0.18) * values
    return jnp.clip(values, min=-bound, max=bound).astype(kind)


def setup_inputs(seed: int = 0, part: int = 0) -> dict:
    keys = jax.random.split(jax.random.key(seed), 8)
    own_keys = jax.random.split(jax.random.fold_in(keys[7], part), 8)
    return {
        "image_query": draw_image_query(jax.random.fold_in(jax.random.fold_in(keys[7], part), 71), part),
        "image_key": draw_image_key(jax.random.fold_in(jax.random.fold_in(keys[7], part), 71), part),
        "image_value": noise(own_keys[2], (HT, WT, D), 1.0, 6.0, ((0, 4), (1, 4))),
        "text_query": draw_text_query(jax.random.fold_in(jax.random.fold_in(keys[7], part), 71), part),
        "text_key": draw_text_key(jax.random.fold_in(jax.random.fold_in(keys[7], part), 71), part),
        "text_value": noise(own_keys[5], (TXT, D), 1.0, 6.0, ((0, 4),)),
        "text_length": jax.random.randint(own_keys[6], (1,), TXT // 4, TXT + 1).astype(jnp.int32),
    }


masked_score = -1.0e30


def attend(queries, key_rows, value_rows, allowed):
    score_scale = 1.0 / (HEAD_DIM ** 0.5)
    scores = jnp.einsum("qhe,khe->hqk", queries.astype(jnp.float32), key_rows.astype(jnp.float32)) * score_scale
    scores = jnp.where(allowed[None], scores, masked_score)
    row_peak = jnp.max(scores, axis=-1, keepdims=True)
    weights = jnp.exp(scores - row_peak)
    row_total = jnp.sum(weights, axis=-1)
    rounded = lax.optimization_barrier(weights.astype(jnp.bfloat16)).astype(jnp.float32)
    numerator = jnp.einsum("hqk,khe->qhe", rounded, value_rows.astype(jnp.float32))
    return (numerator / jnp.transpose(row_total)[:, :, None]).astype(jnp.bfloat16)


def reference(image_query, image_key, image_value, text_query, text_key, text_value, text_length):
    grid_rows = TH * N_HEIGHT
    grid_cols = TW * N_WIDTH
    ext_rows = TH + 2 * RADIUS
    ext_cols = TW + 2 * RADIUS
    score_scale = 1.0 / (HEAD_DIM ** 0.5)
    pad_shape = ((RADIUS, RADIUS), (RADIUS, RADIUS), (0, 0))
    padded_key = jnp.pad(image_key, pad_shape)
    padded_value = jnp.pad(image_value, pad_shape)
    text_allowed = jnp.arange(TXT, dtype=jnp.int32) < text_length[0]
    text_key_heads = text_key.reshape(TXT, HEADS, HEAD_DIM)
    text_value_heads = text_value.reshape(TXT, HEADS, HEAD_DIM)
    query_row = jnp.arange(TH, dtype=jnp.int32)[:, None, None, None]
    query_col = jnp.arange(TW, dtype=jnp.int32)[None, :, None, None]
    key_row = jnp.arange(ext_rows, dtype=jnp.int32)[None, None, :, None]
    key_col = jnp.arange(ext_cols, dtype=jnp.int32)[None, None, None, :]

    def one_tile(tile_index):
        row_base = (tile_index // N_WIDTH) * TH
        col_base = (tile_index % N_WIDTH) * TW
        anchor = jnp.zeros((), jnp.int32)
        queries = lax.dynamic_slice(image_query, (row_base, col_base, anchor), (TH, TW, D)).reshape(TH * TW, HEADS, HEAD_DIM)
        tile_keys = lax.dynamic_slice(padded_key, (row_base, col_base, anchor), (ext_rows, ext_cols, D)).reshape(ext_rows * ext_cols, HEADS, HEAD_DIM)
        tile_values = lax.dynamic_slice(padded_value, (row_base, col_base, anchor), (ext_rows, ext_cols, D)).reshape(ext_rows * ext_cols, HEADS, HEAD_DIM)
        delta_row = key_row - RADIUS - query_row
        delta_col = key_col - RADIUS - query_col
        global_row = row_base + key_row - RADIUS
        global_col = col_base + key_col - RADIUS
        inside = (global_row >= 0) & (global_row < grid_rows) & (global_col >= 0) & (global_col < grid_cols)
        near = delta_row * delta_row + delta_col * delta_col <= RADIUS * RADIUS
        win_allowed = (near & inside).reshape(TH * TW, ext_rows * ext_cols)
        allowed = jnp.concatenate([win_allowed, jnp.broadcast_to(text_allowed[None], (TH * TW, TXT))], axis=1)
        merged_keys = jnp.concatenate([tile_keys, text_key_heads], axis=0)
        merged_values = jnp.concatenate([tile_values, text_value_heads], axis=0)
        return attend(queries, merged_keys, merged_values, allowed).reshape(TH, TW, D)

    tiles = lax.map(one_tile, jnp.arange(N_HEIGHT * N_WIDTH, dtype=jnp.int32))
    image_out = tiles.reshape(N_HEIGHT, N_WIDTH, TH, TW, D).transpose(0, 2, 1, 3, 4).reshape(grid_rows, grid_cols, D)

    query_heads = text_query.reshape(TXT, HEADS, HEAD_DIM).transpose(1, 0, 2)
    image_key_heads = image_key.reshape(grid_rows * grid_cols, HEADS, HEAD_DIM).transpose(1, 0, 2)
    image_value_heads = image_value.reshape(grid_rows * grid_cols, HEADS, HEAD_DIM).transpose(1, 0, 2)
    text_key_major = text_key_heads.transpose(1, 0, 2)
    text_value_major = text_value_heads.transpose(1, 0, 2)

    def one_head(operands):
        head_query, head_key, head_value, head_text_key, head_text_value = operands
        image_scores = jnp.dot(head_query, head_key.T, preferred_element_type=jnp.float32) * score_scale
        text_scores = jnp.dot(head_query, head_text_key.T, preferred_element_type=jnp.float32) * score_scale
        text_scores = jnp.where(text_allowed[None], text_scores, masked_score)
        row_peak = jnp.maximum(jnp.max(image_scores, axis=1), jnp.max(text_scores, axis=1))[:, None]
        image_weight = jnp.exp(image_scores - row_peak)
        text_weight = jnp.exp(text_scores - row_peak)
        row_total = jnp.sum(image_weight, axis=1) + jnp.sum(text_weight, axis=1)
        numerator = jnp.dot(image_weight.astype(jnp.bfloat16), head_value, preferred_element_type=jnp.float32)
        numerator = numerator + jnp.dot(text_weight.astype(jnp.bfloat16), head_text_value, preferred_element_type=jnp.float32)
        return numerator / row_total[:, None]

    heads_out = lax.map(one_head, (query_heads, image_key_heads, image_value_heads, text_key_major, text_value_major))
    text_out = heads_out.transpose(1, 0, 2).reshape(TXT, D).astype(jnp.bfloat16)
    return (image_out, text_out)
```

```python
import functools
import math

import jax
import jax.numpy as jnp
from jax import lax
from jax.experimental import pallas as pl
from jax.experimental.pallas import tpu as pltpu
from jax.sharding import PartitionSpec as P

HEAD_DIM = 128
RADIUS = 8
CHUNKS = 4
MASKED = -1e30
SCALE = math.log2(math.e) / math.sqrt(HEAD_DIM)
NT = (((1,), (1,)), ((), ()))


def dot_nt(a, b):
    return lax.dot_general(a, b, NT, preferred_element_type=jnp.float32)


def dot_nn(a, b):
    return jnp.dot(a, b, preferred_element_type=jnp.float32)


def joint(
    dims,
    length_ref,
    q_ref,
    k_hbm,
    v_hbm,
    tq_hbm,
    tk_hbm,
    tv_hbm,
    image_out,
    text_out,
    kbuf,
    vbuf,
    tk,
    tv,
    tq,
    xk,
    xv,
    obuf,
    rbuf,
    tout,
    bias,
    local_sem,
    zs,
    zr,
    vs,
    vr,
    ts,
    tr,
    ps,
    pr,
    qs,
    qr,
    xs,
    xr,
    os_,
    or_,
    fs,
    fr,
):
    n_h, n_w, rows, cols, heads, own_text, parts = dims
    tile = rows * cols
    strip = RADIUS * cols
    text = own_text * n_w
    groups = n_h // parts
    part_heads = heads // parts
    pc = part_heads * HEAD_DIM
    chunk_heads = heads // CHUNKS
    cc = chunk_heads * HEAD_DIM
    hc = cc // 2
    h = lax.axis_index("height")
    w = lax.axis_index("width")
    group = lax.div(h, parts)
    part = lax.rem(h, parts)
    par = lax.rem(h, 2)
    has_left, has_right = w > 0, w < n_w - 1
    has_up, has_down = h > 0, h < n_h - 1

    def at(hh, ww):
        return {"height": hh, "width": ww}

    def send(src, dst, s, r, device):
        return pltpu.make_async_remote_copy(
            src_ref=src,
            dst_ref=dst,
            send_sem=s,
            recv_sem=r,
            device_id=device,
            device_id_type=pl.DeviceIdType.MESH,
        )

    images = ((k_hbm, kbuf), (v_hbm, vbuf))
    texts = ((tk_hbm, tk), (tv_hbm, tv))
    part_cols = pl.ds(pl.multiple_of(part * pc, 128), pc)
    my_rows = pl.ds(pl.multiple_of(w * own_text, 16), own_text)

    barrier = pltpu.get_barrier_semaphore()
    greeted = 0
    for d in range(1, n_w):
        pl.semaphore_signal(barrier, inc=1, device_id=at(h, lax.rem(w + d, n_w)), device_id_type=pl.DeviceIdType.MESH)
        greeted += 1
    for d in range(1, n_h):
        pl.semaphore_signal(barrier, inc=1, device_id=at(lax.rem(h + d, n_h), w), device_id_type=pl.DeviceIdType.MESH)
        greeted += 1
    for g in range(1, groups):
        for d in range(1, n_w):
            pl.semaphore_signal(
                barrier,
                inc=1,
                device_id=at(lax.rem(h + g * parts, n_h), lax.rem(w + d, n_w)),
                device_id_type=pl.DeviceIdType.MESH,
            )
            greeted += 1
    pl.semaphore_wait(barrier, greeted)

    locals_ = []
    for i, (src, dst) in enumerate(images):
        locals_.append(pltpu.make_async_copy(src, dst.at[pl.ds(0, tile), :], local_sem.at[i]))
    locals_.append(pltpu.make_async_copy(tq_hbm.at[:, part_cols], tq.at[my_rows, :], local_sem.at[2]))
    my_slot = pl.ds(pl.multiple_of(part * tile, 16), tile)
    for i, (src, dst) in enumerate(((k_hbm, xk), (v_hbm, xv))):
        locals_.append(pltpu.make_async_copy(src.at[:, part_cols], dst.at[my_slot, :], local_sem.at[3 + i]))

    def half_cols(c):
        return pl.ds(pl.multiple_of(c * cc + par * hc, 128), hc)

    for c in range(CHUNKS):
        for i, (src, dst) in enumerate(texts):
            locals_.append(
                pltpu.make_async_copy(
                    src.at[:, half_cols(c)], dst.at[my_rows, half_cols(c)], local_sem.at[5 + 2 * c + i]
                )
            )
    for copy in locals_:
        copy.start()

    q_sends = [
        send(tq_hbm.at[:, part_cols], tq.at[my_rows, :], qs.at[d], qr.at[d], at(h, lax.rem(w + d, n_w)))
        for d in range(1, n_w)
    ]
    x_sends = []
    for d in range(1, parts):
        other = lax.rem(part + d, parts)
        other_cols = pl.ds(pl.multiple_of(other * pc, 128), pc)
        for i, (src, dst) in enumerate(((k_hbm, xk), (v_hbm, xv))):
            x_sends.append(
                send(src.at[:, other_cols], dst.at[my_slot, :], xs.at[d, i], xr.at[d, i], at(group * parts + other, w))
            )

    def text_sends(c):
        return [
            send(
                src.at[:, half_cols(c)],
                dst.at[my_rows, half_cols(c)],
                ts.at[c, d, i],
                tr.at[c, d, i],
                at(h, lax.rem(w + d, n_w)),
            )
            for d in range(1, n_w)
            for i, (src, dst) in enumerate(texts)
        ]

    def pair_sends(c):
        partner = h + 1 - 2 * par
        return [
            send(dst.at[:, half_cols(c)], dst.at[:, half_cols(c)], ps.at[c, i], pr.at[c, i], at(partner, w))
            for i, (_, dst) in enumerate(texts)
        ]

    def side_sends(c, way):
        to = w + 1 if way == 0 else w - 1
        columns = pl.ds(c * cc, cc)
        return [
            send(
                src.at[:, columns],
                dst.at[pl.ds(tile * (1 + way), tile), columns],
                zs.at[c, way, i],
                zr.at[c, way, i],
                at(h, to),
            )
            for i, (src, dst) in enumerate(images)
        ]

    def strip_sends(c, way, piece):
        to = h + 1 if way == 0 else h - 1
        columns = pl.ds(c * cc, cc)
        start = tile - strip if way == 0 else 0
        slot = 3 * tile + (3 * way + piece) * strip
        return [
            send(
                (src if piece == 0 else dst).at[pl.ds(piece * tile + start, strip), columns],
                dst.at[pl.ds(slot, strip), columns],
                vs.at[c, way, piece, i],
                vr.at[c, way, piece, i],
                at(to, w),
            )
            for i, (src, dst) in enumerate(images)
        ]

    side_out = (has_right, has_left)
    side_in = (has_left, has_right)
    strip_out = (has_down, has_up)
    strip_in = (has_up, has_down)
    piece_there = (True, has_left, has_right)

    def start_chunk(c):
        for copy in text_sends(c):
            copy.start()
        for way in range(2):

            @pl.when(side_out[way])
            def _(way=way):
                for copy in side_sends(c, way):
                    copy.start()

            @pl.when(strip_out[way])
            def _(way=way):
                for copy in strip_sends(c, way, 0):
                    copy.start()

    def relay_chunk(c):
        for copy in text_sends(c):
            copy.wait_recv()
        for i in range(2):
            locals_[5 + 2 * c + i].wait()
        for copy in pair_sends(c):
            copy.start()
        for way in range(2):

            @pl.when(side_in[way])
            def _(way=way):
                for copy in side_sends(c, way):
                    copy.wait_recv()
                for up in range(2):

                    @pl.when(strip_out[up])
                    def _():
                        for copy in strip_sends(c, up, 1 + way):
                            copy.start()

    def wait_chunk(c):
        for copy in pair_sends(c):
            copy.wait_recv()
        for way in range(2):
            for piece in range(3):

                @pl.when(strip_in[way] & piece_there[piece])
                def _(way=way, piece=piece):
                    for copy in strip_sends(c, way, piece):
                        copy.wait_recv()

    def finish_chunk(c):
        for copy in text_sends(c) + pair_sends(c):
            copy.wait_send()
        for way in range(2):

            @pl.when(side_out[way])
            def _(way=way):
                for copy in side_sends(c, way):
                    copy.wait_send()

            for piece in range(3):

                @pl.when(strip_out[way] & piece_there[piece])
                def _(way=way, piece=piece):
                    for copy in strip_sends(c, way, piece):
                        copy.wait_send()

    for copy in q_sends + x_sends:
        copy.start()
    start_chunk(0)
    start_chunk(1)

    def region(first, count, row_off, col_off, valid):
        key = lax.broadcasted_iota(jnp.int32, (tile, count), 1)
        query = lax.broadcasted_iota(jnp.int32, (tile, count), 0)
        delta_row = lax.div(key, cols) + row_off - lax.div(query, cols)
        delta_col = lax.rem(key, cols) + col_off - lax.rem(query, cols)
        near = delta_row * delta_row + delta_col * delta_col <= RADIUS * RADIUS
        limit = jnp.where(valid, 0.0, MASKED)
        bias[:, first : first + count] = jnp.where(near, limit, MASKED)

    region(0, tile, 0, 0, True)
    region(tile, tile, 0, -cols, has_left)
    region(2 * tile, tile, 0, cols, has_right)
    for way in range(2):
        row_off = -RADIUS if way == 0 else rows
        for piece in range(3):
            col_off = (0, -cols, cols)[piece]
            first = 3 * tile + (3 * way + piece) * strip
            region(first, strip, row_off, col_off, strip_in[way] & piece_there[piece])

            @pl.when(jnp.logical_not(strip_in[way] & piece_there[piece]))
            def _():
                for _, dst in images:
                    dst[first : first + strip, :] = jnp.zeros((strip, dst.shape[1]), dst.dtype)

        @pl.when(jnp.logical_not(side_in[way]))
        def _():
            for _, dst in images:
                first = tile * (1 + way)
                dst[first : first + tile, :] = jnp.zeros((tile, dst.shape[1]), dst.dtype)

    def text_bias():
        return jnp.where(lax.broadcasted_iota(jnp.int32, (1, text), 1) < length_ref[0], 0.0, MASKED)

    def attend_chunk(c):
        limit = text_bias()

        def one_head(j, carry):
            column = pl.ds(pl.multiple_of(c * cc + j * HEAD_DIM, 128), HEAD_DIM)
            query = q_ref[:, column]
            score_win = dot_nt(query, kbuf[:, column]) + bias[...]
            score_text = dot_nt(query, tk[:, column]) + limit
            peak = jnp.maximum(
                jnp.max(score_win, axis=1, keepdims=True), jnp.max(score_text, axis=1, keepdims=True)
            )
            weight_win = jnp.exp2((score_win - peak) * SCALE)
            weight_text = jnp.exp2((score_text - peak) * SCALE)
            total = jnp.sum(weight_win, axis=1, keepdims=True) + jnp.sum(weight_text, axis=1, keepdims=True)
            numer = dot_nn(weight_win.astype(jnp.bfloat16), vbuf[:, column])
            numer = numer + dot_nn(weight_text.astype(jnp.bfloat16), tv[:, column])
            image_out[:, column] = (numer / total).astype(jnp.bfloat16)
            return carry

        lax.fori_loop(0, chunk_heads, one_head, 0, unroll=2)

    block = math.gcd(text, 128)

    def text_partial(b, carry):
        block_rows = pl.ds(pl.multiple_of(b * block, block), block)
        lane = lax.broadcasted_iota(jnp.int32, (block, 128), 1)
        stats = jnp.zeros((block, 128), jnp.float32)
        for j in range(part_heads):
            column = slice(j * HEAD_DIM, (j + 1) * HEAD_DIM)
            score = dot_nt(tq[block_rows, column], xk[:, column])
            peak = jnp.max(score, axis=1, keepdims=True)
            weight = jnp.exp2((score - peak) * SCALE)
            total = jnp.sum(weight, axis=1, keepdims=True)
            obuf[block_rows, column] = dot_nn(weight.astype(jnp.bfloat16), xv[:, column])
            stats = jnp.where(lane == j, peak, jnp.where(lane == 64 + j, total, stats))
        obuf[block_rows, pc : pc + 128] = stats
        return carry

    o_sends = []
    for g in range(groups):
        for d in range(n_w):
            if g or d:
                to_w = lax.rem(w + d, n_w)
                their_rows = pl.ds(pl.multiple_of(to_w * own_text, 16), own_text)
                at_slot = g * n_w + d
                o_sends.append(
                    send(
                        obuf.at[their_rows, :],
                        rbuf.at[at_slot],
                        os_.at[at_slot],
                        or_.at[at_slot],
                        at(lax.rem(h + g * parts, n_h), to_w),
                    )
                )

    f_sends = [
        send(
            tout.at[:, part_cols],
            tout.at[:, part_cols],
            fs.at[d],
            fr.at[d],
            at(group * parts + lax.rem(part + d, parts), w),
        )
        for d in range(1, parts)
    ]

    def text_combine():
        limit = text_bias()
        for j in range(part_heads):
            column = slice(j * HEAD_DIM, (j + 1) * HEAD_DIM)
            wide = pl.ds(pl.multiple_of(part * pc + j * HEAD_DIM, 128), HEAD_DIM)
            score = dot_nt(tq[my_rows, column], tk[:, wide]) + limit
            own_peak = jnp.max(score, axis=1, keepdims=True)
            pieces = [(obuf[my_rows, column], obuf[my_rows, pc : pc + 128])]
            for s in range(1, groups * n_w):
                pieces.append((rbuf[s, :, column], rbuf[s, :, pc : pc + 128]))
            peak = own_peak
            for _, stats in pieces:
                peak = jnp.maximum(peak, stats[:, j : j + 1])
            weight = jnp.exp2((score - peak) * SCALE)
            total = jnp.sum(weight, axis=1, keepdims=True)
            numer = dot_nn(weight.astype(jnp.bfloat16), tv[:, wide])
            for value, stats in pieces:
                factor = jnp.exp2((stats[:, j : j + 1] - peak) * SCALE)
                total = total + factor * stats[:, 64 + j : 65 + j]
                numer = numer + factor * value
            tout[:, wide] = (numer / total).astype(jnp.bfloat16)

    for i in range(2):
        locals_[i].wait()
    for c in range(CHUNKS):
        relay_chunk(c)
        if c + 2 < CHUNKS:
            start_chunk(c + 2)
        if c == 0:
            for copy in q_sends + x_sends:
                copy.wait_recv()
            for i in range(2, 5):
                locals_[i].wait()
            lax.fori_loop(0, text // block, text_partial, 0)
            for copy in o_sends:
                copy.start()
        else:
            wait_chunk(c - 1)
            attend_chunk(c - 1)
    last = CHUNKS - 1
    for copy in pair_sends(last):
        copy.wait_recv()
    for copy in o_sends:
        copy.wait_recv()
    text_combine()
    for copy in f_sends:
        copy.start()
    for way in range(2):
        for piece in range(3):

            @pl.when(strip_in[way] & piece_there[piece])
            def _(way=way, piece=piece):
                for copy in strip_sends(last, way, piece):
                    copy.wait_recv()

    attend_chunk(last)
    for copy in f_sends:
        copy.wait_recv()
    text_out[...] = tout[...]
    for copy in q_sends + x_sends + o_sends + f_sends:
        copy.wait_send()
    for c in range(CHUNKS):
        finish_chunk(c)


def shards(image_query, image_key, image_value, text_query, text_key, text_value, text_length):
    rows, cols, width = image_query.shape
    heads = width // HEAD_DIM
    n_h, n_w = lax.axis_size("height"), lax.axis_size("width")
    own_text = text_query.shape[0]
    parts = math.gcd(heads, n_h)
    tile = rows * cols
    strip = RADIUS * cols
    text = own_text * n_w
    sources = (n_h // parts) * n_w
    pc = width // parts
    keys = 3 * tile + 6 * strip
    bf16, f32 = jnp.bfloat16, jnp.float32
    dma = pltpu.SemaphoreType.DMA
    any_spec = pl.BlockSpec(memory_space=pl.ANY)
    vmem_spec = pl.BlockSpec(memory_space=pltpu.VMEM)
    image_out, text_out = pl.pallas_call(
        functools.partial(joint, (n_h, n_w, rows, cols, heads, own_text, parts)),
        out_shape=(
            jax.ShapeDtypeStruct((tile, width), bf16),
            jax.ShapeDtypeStruct((own_text, width), bf16),
        ),
        in_specs=[pl.BlockSpec(memory_space=pltpu.SMEM), vmem_spec] + [any_spec] * 5,
        out_specs=(vmem_spec, vmem_spec),
        scratch_shapes=[
            pltpu.VMEM((keys, width), bf16),
            pltpu.VMEM((keys, width), bf16),
            pltpu.VMEM((text, width), bf16),
            pltpu.VMEM((text, width), bf16),
            pltpu.VMEM((text, pc), bf16),
            pltpu.VMEM((parts * tile, pc), bf16),
            pltpu.VMEM((parts * tile, pc), bf16),
            pltpu.VMEM((text, pc + 128), f32),
            pltpu.VMEM((sources, own_text, pc + 128), f32),
            pltpu.VMEM((own_text, width), bf16),
            pltpu.VMEM((tile, keys), f32),
            dma((5 + 2 * CHUNKS,)),
            dma((CHUNKS, 2, 2)),
            dma((CHUNKS, 2, 2)),
            dma((CHUNKS, 2, 3, 2)),
            dma((CHUNKS, 2, 3, 2)),
            dma((CHUNKS, n_w, 2)),
            dma((CHUNKS, n_w, 2)),
            dma((CHUNKS, 2)),
            dma((CHUNKS, 2)),
            dma((n_w,)),
            dma((n_w,)),
            dma((parts, 2)),
            dma((parts, 2)),
            dma((sources,)),
            dma((sources,)),
            dma((parts,)),
            dma((parts,)),
        ],
        compiler_params=pltpu.CompilerParams(
            collective_id=0, has_side_effects=True, vmem_limit_bytes=50 * 1024 * 1024
        ),
        cost_estimate=pl.CostEstimate(
            flops=4 * tile * (keys + 2 * text) * width,
            bytes_accessed=12 * tile * width,
            transcendentals=heads * tile * (keys + 2 * text),
        ),
        name="joint_attention",
    )(
        text_length,
        image_query.reshape(tile, width),
        image_key.reshape(tile, width),
        image_value.reshape(tile, width),
        text_query,
        text_key,
        text_value,
    )
    return image_out.reshape(rows, cols, width), text_out


def solution(mesh):
    in_specs = (
        P(("batch", "height"), "width", None),
        P(("batch", "height"), "width", None),
        P(("batch", "height"), "width", None),
        P(("batch", "width"), None),
        P(("batch", "width"), None),
        P(("batch", "width"), None),
        P("batch"),
    )
    out_specs = (P(("batch", "height"), "width", None), P(("batch", "width"), None))
    return jax.shard_map(shards, mesh=mesh, in_specs=in_specs, out_specs=out_specs, check_vma=False)
```

```python
import functools
import math

import jax
import jax.numpy as jnp
from jax import lax
from jax.experimental import pallas as pl
from jax.experimental.pallas import tpu as pltpu
from jax.sharding import PartitionSpec as P

HEAD_DIM = 128
RADIUS = 8
CHUNKS = 4
MASKED = -1e30
VMEM_BYTES = 62 * 1024 * 1024
SCALE = math.log2(math.e) / math.sqrt(HEAD_DIM)
NT = (((1,), (1,)), ((), ()))


def dot_nt(a, b):
    return lax.dot_general(a, b, NT, preferred_element_type=jnp.float32)


def dot_nn(a, b):
    return jnp.dot(a, b, preferred_element_type=jnp.float32)


def joint(
    dims,
    length_ref,
    q_hbm,
    k_hbm,
    v_hbm,
    tq_hbm,
    tk_hbm,
    tv_hbm,
    image_out,
    text_out,
    q_ref,
    kbuf,
    vbuf,
    tk,
    tv,
    tq,
    xk,
    xv,
    obuf,
    rbuf,
    tout,
    bias,
    local_sem,
    zs,
    zr,
    vs,
    vr,
    ts,
    tr,
    ps,
    pr,
    xs,
    xr,
    os_,
    or_,
    fs,
    fr,
):
    n_h, n_w, rows, cols, heads, own_text, parts = dims
    tile = rows * cols
    strip = RADIUS * cols
    text = own_text * n_w
    groups = n_h // parts
    part_heads = heads // parts
    pc = part_heads * HEAD_DIM
    chunk_heads = heads // CHUNKS
    cc = chunk_heads * HEAD_DIM
    hc = cc // 2
    h = lax.axis_index("height")
    w = lax.axis_index("width")
    group = lax.div(h, parts)
    part = lax.rem(h, parts)
    par = lax.rem(h, 2)
    has_left, has_right = w > 0, w < n_w - 1
    has_up, has_down = h > 0, h < n_h - 1

    def at(hh, ww):
        return {"height": hh, "width": ww}

    def send(src, dst, s, r, device):
        return pltpu.make_async_remote_copy(
            src_ref=src,
            dst_ref=dst,
            send_sem=s,
            recv_sem=r,
            device_id=device,
            device_id_type=pl.DeviceIdType.MESH,
        )

    images = ((k_hbm, kbuf), (v_hbm, vbuf))
    texts = ((tk_hbm, tk), (tv_hbm, tv))
    part_cols = pl.ds(pl.multiple_of(part * pc, 128), pc)
    my_rows = pl.ds(pl.multiple_of(w * own_text, 16), own_text)

    barrier = pltpu.get_barrier_semaphore()
    greeted = 0
    for d in range(1, n_w):
        pl.semaphore_signal(barrier, inc=1, device_id=at(h, lax.rem(w + d, n_w)), device_id_type=pl.DeviceIdType.MESH)
        greeted += 1
    for d in range(1, n_h):
        pl.semaphore_signal(barrier, inc=1, device_id=at(lax.rem(h + d, n_h), w), device_id_type=pl.DeviceIdType.MESH)
        greeted += 1
    for g in range(1, groups):
        for d in range(1, n_w):
            pl.semaphore_signal(
                barrier,
                inc=1,
                device_id=at(lax.rem(h + g * parts, n_h), lax.rem(w + d, n_w)),
                device_id_type=pl.DeviceIdType.MESH,
            )
            greeted += 1
    pl.semaphore_wait(barrier, greeted)

    locals_ = []
    for i, (src, dst) in enumerate(images):
        locals_.append(pltpu.make_async_copy(src, dst.at[pl.ds(0, tile), :], local_sem.at[i]))
    my_slot = pl.ds(pl.multiple_of(part * tile, 16), tile)
    for i, (src, dst) in enumerate(((k_hbm, xk), (v_hbm, xv))):
        locals_.append(pltpu.make_async_copy(src.at[:, part_cols], dst.at[my_slot, :], local_sem.at[2 + i]))

    slabs = ((tq_hbm, tq, pl.ds(0, pc)), (tk_hbm, tk, part_cols), (tv_hbm, tv, part_cols))
    for i, (src, dst, columns) in enumerate(slabs):
        locals_.append(pltpu.make_async_copy(src.at[:, part_cols], dst.at[my_rows, columns], local_sem.at[4 + i]))
    locals_.append(pltpu.make_async_copy(q_hbm, q_ref, local_sem.at[7]))
    for copy in locals_:
        copy.start()

    def slab_sends(hop, way):
        owner = w - hop if way == 0 else w + hop
        owner_rows = pl.ds(pl.multiple_of(owner * own_text, 16), own_text)
        to = w + 1 if way == 0 else w - 1
        return [
            send(
                src.at[:, part_cols] if hop == 0 else dst.at[owner_rows, columns],
                dst.at[owner_rows, columns],
                ts.at[hop, way, i],
                tr.at[hop, way, i],
                at(h, to),
            )
            for i, (src, dst, columns) in enumerate(slabs)
        ]

    def slab_in(hop, way):
        return w > hop if way == 0 else w < n_w - 1 - hop

    def flipped(bit):
        return part + bit * (1 - 2 * lax.rem(lax.div(part, bit), 2))

    exchanges = []
    offsets = [0]
    bit = parts // 2
    while bit:
        stage = []
        for offset in offsets:
            held = part
            for b in range(8):
                if offset & (1 << b):
                    held = held + (1 << b) * (1 - 2 * lax.rem(lax.div(part, 1 << b), 2))
            columns = pl.ds(pl.multiple_of(held * pc, 128), pc)
            for i, (_, dst) in enumerate(texts):
                at_sem = len(offsets) + len(stage) // 2
                stage.append(
                    send(
                        dst.at[:, columns],
                        dst.at[:, columns],
                        ps.at[at_sem, i],
                        pr.at[at_sem, i],
                        at(group * parts + flipped(bit), w),
                    )
                )
        exchanges.append(stage)
        offsets = offsets + [o ^ bit for o in offsets]
        bit //= 2

    x_sends = []
    for d in range(1, parts):
        other = lax.rem(part + d, parts)
        other_cols = pl.ds(pl.multiple_of(other * pc, 128), pc)
        for i, (src, dst) in enumerate(((k_hbm, xk), (v_hbm, xv))):
            x_sends.append(
                send(src.at[:, other_cols], dst.at[my_slot, :], xs.at[d, i], xr.at[d, i], at(group * parts + other, w))
            )

    def side_sends(c, way):
        to = w + 1 if way == 0 else w - 1
        columns = pl.ds(c * cc, cc)
        return [
            send(
                src.at[:, columns],
                dst.at[pl.ds(tile * (1 + way), tile), columns],
                zs.at[c, way, i],
                zr.at[c, way, i],
                at(h, to),
            )
            for i, (src, dst) in enumerate(images)
        ]

    def strip_sends(c, way, piece):
        to = h + 1 if way == 0 else h - 1
        columns = pl.ds(c * cc, cc)
        start = tile - strip if way == 0 else 0
        slot = 3 * tile + (3 * way + piece) * strip
        return [
            send(
                (src if piece == 0 else dst).at[pl.ds(piece * tile + start, strip), columns],
                dst.at[pl.ds(slot, strip), columns],
                vs.at[c, way, piece, i],
                vr.at[c, way, piece, i],
                at(to, w),
            )
            for i, (src, dst) in enumerate(images)
        ]

    side_out = (has_right, has_left)
    side_in = (has_left, has_right)
    strip_out = (has_down, has_up)
    strip_in = (has_up, has_down)
    piece_there = (True, has_left, has_right)

    def start_chunk(c):
        for way in range(2):

            @pl.when(side_out[way])
            def _(way=way):
                for copy in side_sends(c, way):
                    copy.start()

            @pl.when(strip_out[way])
            def _(way=way):
                for copy in strip_sends(c, way, 0):
                    copy.start()

    def relay_chunk(c):
        for way in range(2):

            @pl.when(side_in[way])
            def _(way=way):
                for copy in side_sends(c, way):
                    copy.wait_recv()
                for up in range(2):

                    @pl.when(strip_out[up])
                    def _():
                        for copy in strip_sends(c, up, 1 + way):
                            copy.start()

    def wait_chunk(c):
        for way in range(2):
            for piece in range(3):

                @pl.when(strip_in[way] & piece_there[piece])
                def _(way=way, piece=piece):
                    for copy in strip_sends(c, way, piece):
                        copy.wait_recv()

    def finish_chunk(c):
        for way in range(2):

            @pl.when(side_out[way])
            def _(way=way):
                for copy in side_sends(c, way):
                    copy.wait_send()

            for piece in range(3):

                @pl.when(strip_out[way] & piece_there[piece])
                def _(way=way, piece=piece):
                    for copy in strip_sends(c, way, piece):
                        copy.wait_send()

    for way in range(2):

        @pl.when(side_out[way])
        def _(way=way):
            for copy in slab_sends(0, way):
                copy.start()

    for copy in x_sends:
        copy.start()
    start_chunk(0)
    start_chunk(1)

    def region(first, count, row_off, col_off, valid):
        key = lax.broadcasted_iota(jnp.int32, (tile, count), 1)
        query = lax.broadcasted_iota(jnp.int32, (tile, count), 0)
        delta_row = lax.div(key, cols) + row_off - lax.div(query, cols)
        delta_col = lax.rem(key, cols) + col_off - lax.rem(query, cols)
        near = delta_row * delta_row + delta_col * delta_col <= RADIUS * RADIUS
        limit = jnp.where(valid, 0.0, MASKED)
        bias[:, first : first + count] = jnp.where(near, limit, MASKED)

    region(0, tile, 0, 0, True)
    region(tile, tile, 0, -cols, has_left)
    region(2 * tile, tile, 0, cols, has_right)
    for way in range(2):
        row_off = -RADIUS if way == 0 else rows
        for piece in range(3):
            col_off = (0, -cols, cols)[piece]
            first = 3 * tile + (3 * way + piece) * strip
            region(first, strip, row_off, col_off, strip_in[way] & piece_there[piece])

            @pl.when(jnp.logical_not(strip_in[way] & piece_there[piece]))
            def _():
                for _, dst in images:
                    dst[first : first + strip, :] = jnp.zeros((strip, dst.shape[1]), dst.dtype)

        @pl.when(jnp.logical_not(side_in[way]))
        def _():
            for _, dst in images:
                first = tile * (1 + way)
                dst[first : first + tile, :] = jnp.zeros((tile, dst.shape[1]), dst.dtype)

    def text_bias():
        return jnp.where(lax.broadcasted_iota(jnp.int32, (1, text), 1) < length_ref[0], 0.0, MASKED)

    def attend_chunk(c):
        limit = text_bias()

        def one_head(j, carry):
            column = pl.ds(pl.multiple_of(c * cc + j * HEAD_DIM, 128), HEAD_DIM)
            query = q_ref[:, column]
            score_win = dot_nt(query, kbuf[:, column]) + bias[...]
            score_text = dot_nt(query, tk[:, column]) + limit
            peak = jnp.maximum(
                jnp.max(score_win, axis=1, keepdims=True), jnp.max(score_text, axis=1, keepdims=True)
            )
            weight_win = jnp.exp2((score_win - peak) * SCALE)
            weight_text = jnp.exp2((score_text - peak) * SCALE)
            total = jnp.sum(weight_win, axis=1, keepdims=True) + jnp.sum(weight_text, axis=1, keepdims=True)
            numer = dot_nn(weight_win.astype(jnp.bfloat16), vbuf[:, column])
            numer = numer + dot_nn(weight_text.astype(jnp.bfloat16), tv[:, column])
            image_out[:, column] = (numer / total).astype(jnp.bfloat16)
            return carry

        lax.fori_loop(0, chunk_heads, one_head, 0, unroll=2)

    block = math.gcd(text, 128)

    def text_partial(b, carry):
        block_rows = pl.ds(pl.multiple_of(b * block, block), block)
        lane = lax.broadcasted_iota(jnp.int32, (block, 128), 1)
        stats = jnp.zeros((block, 128), jnp.float32)
        for j in range(part_heads):
            column = slice(j * HEAD_DIM, (j + 1) * HEAD_DIM)
            score = dot_nt(tq[block_rows, column], xk[:, column])
            peak = jnp.max(score, axis=1, keepdims=True)
            weight = jnp.exp2((score - peak) * SCALE)
            total = jnp.sum(weight, axis=1, keepdims=True)
            numer = dot_nn(weight.astype(jnp.bfloat16), xv[:, column])
            obuf[block_rows, column] = (numer / total).astype(jnp.bfloat16)
            log_total = peak * SCALE + jnp.log2(total)
            for third in range(3):
                piece = log_total.astype(jnp.bfloat16).astype(jnp.float32)
                stats = jnp.where(lane == 32 * third + j, piece, stats)
                log_total = log_total - piece
        obuf[block_rows, pc : pc + 128] = stats.astype(jnp.bfloat16)
        return carry

    o_sends = []
    for g in range(groups):
        for d in range(n_w):
            if g or d:
                to_w = lax.rem(w + d, n_w)
                their_rows = pl.ds(pl.multiple_of(to_w * own_text, 16), own_text)
                at_slot = g * n_w + d
                o_sends.append(
                    send(
                        obuf.at[their_rows, :],
                        rbuf.at[at_slot],
                        os_.at[at_slot],
                        or_.at[at_slot],
                        at(lax.rem(h + g * parts, n_h), to_w),
                    )
                )

    f_sends = [
        send(
            tout.at[:, part_cols],
            tout.at[:, part_cols],
            fs.at[d],
            fr.at[d],
            at(group * parts + lax.rem(part + d, parts), w),
        )
        for d in range(1, parts)
    ]

    def text_combine():
        limit = text_bias()
        for j in range(part_heads):
            column = slice(j * HEAD_DIM, (j + 1) * HEAD_DIM)
            wide = pl.ds(pl.multiple_of(part * pc + j * HEAD_DIM, 128), HEAD_DIM)
            score = dot_nt(tq[my_rows, column], tk[:, wide]) + limit
            pieces = [(obuf[my_rows, column], obuf[my_rows, pc : pc + 128])]
            for s in range(1, groups * n_w):
                pieces.append((rbuf[s, :, column], rbuf[s, :, pc : pc + 128]))
            logs = []
            for _, stats in pieces:
                stats = stats.astype(jnp.float32)
                logs.append(stats[:, j : j + 1] + stats[:, 32 + j : 33 + j] + stats[:, 64 + j : 65 + j])
            peak = jnp.max(score, axis=1, keepdims=True) * SCALE
            for log_total in logs:
                peak = jnp.maximum(peak, log_total)
            weight = jnp.exp2(score * SCALE - peak)
            total = jnp.sum(weight, axis=1, keepdims=True)
            numer = dot_nn(weight.astype(jnp.bfloat16), tv[:, wide])
            for (value, _), log_total in zip(pieces, logs):
                factor = jnp.exp2(log_total - peak)
                total = total + factor
                numer = numer + factor * value.astype(jnp.float32)
            tout[:, wide] = (numer / total).astype(jnp.bfloat16)

    for copy in locals_:
        copy.wait()
    for hop in range(n_w - 1):
        for way in range(2):

            @pl.when(slab_in(hop, way))
            def _(way=way, hop=hop):
                for copy in slab_sends(hop, way):
                    copy.wait_recv()

            if hop + 1 < n_w - 1:

                @pl.when(slab_in(hop, way) & side_out[way])
                def _(way=way, hop=hop):
                    for copy in slab_sends(hop + 1, way):
                        copy.start()

    def run_exchange(k):
        if k > 0:
            for copy in exchanges[k - 1]:
                copy.wait_recv()
        if k < len(exchanges):
            for copy in exchanges[k]:
                copy.start()

    run_exchange(0)
    relay_chunk(0)
    start_chunk(2)
    for copy in x_sends:
        copy.wait_recv()
    lax.fori_loop(0, text // block, text_partial, 0)
    for copy in o_sends:
        copy.start()
    run_exchange(1)
    relay_chunk(1)
    start_chunk(3)
    for k in range(2, len(exchanges) + 1):
        run_exchange(k)
    wait_chunk(0)
    attend_chunk(0)
    relay_chunk(2)
    wait_chunk(1)
    attend_chunk(1)
    relay_chunk(3)
    for copy in o_sends:
        copy.wait_recv()
    text_combine()
    for copy in f_sends:
        copy.start()
    wait_chunk(2)
    attend_chunk(2)
    wait_chunk(3)
    attend_chunk(3)
    for copy in f_sends:
        copy.wait_recv()
    text_out[...] = tout[...]
    for stage in exchanges:
        for copy in stage:
            copy.wait_send()
    for copy in x_sends + o_sends + f_sends:
        copy.wait_send()
    for way in range(2):

        @pl.when(side_out[way])
        def _(way=way):
            for copy in slab_sends(0, way):
                copy.wait_send()

        for hop in range(1, n_w - 1):

            @pl.when(slab_in(hop - 1, way) & side_out[way])
            def _(way=way, hop=hop):
                for copy in slab_sends(hop, way):
                    copy.wait_send()

    for c in range(CHUNKS):
        finish_chunk(c)


def shards(image_query, image_key, image_value, text_query, text_key, text_value, text_length):
    rows, cols, width = image_query.shape
    heads = width // HEAD_DIM
    n_h, n_w = lax.axis_size("height"), lax.axis_size("width")
    own_text = text_query.shape[0]
    parts = math.gcd(math.gcd(heads, n_h), 8)
    tile = rows * cols
    strip = RADIUS * cols
    text = own_text * n_w
    sources = (n_h // parts) * n_w
    pc = width // parts
    keys = 3 * tile + 6 * strip
    bf16, f32 = jnp.bfloat16, jnp.float32
    dma = pltpu.SemaphoreType.DMA
    any_spec = pl.BlockSpec(memory_space=pl.ANY)
    vmem_spec = pl.BlockSpec(memory_space=pltpu.VMEM)
    image_out, text_out = pl.pallas_call(
        functools.partial(joint, (n_h, n_w, rows, cols, heads, own_text, parts)),
        out_shape=(
            jax.ShapeDtypeStruct((tile, width), bf16),
            jax.ShapeDtypeStruct((own_text, width), bf16),
        ),
        in_specs=[pl.BlockSpec(memory_space=pltpu.SMEM)] + [any_spec] * 6,
        out_specs=(vmem_spec, vmem_spec),
        scratch_shapes=[
            pltpu.VMEM((tile, width), bf16),
            pltpu.VMEM((keys, width), bf16),
            pltpu.VMEM((keys, width), bf16),
            pltpu.VMEM((text, width), bf16),
            pltpu.VMEM((text, width), bf16),
            pltpu.VMEM((text, pc), bf16),
            pltpu.VMEM((parts * tile, pc), bf16),
            pltpu.VMEM((parts * tile, pc), bf16),
            pltpu.VMEM((text, pc + 128), bf16),
            pltpu.VMEM((sources, own_text, pc + 128), bf16),
            pltpu.VMEM((own_text, width), bf16),
            pltpu.VMEM((tile, keys), f32),
            dma((8,)),
            dma((CHUNKS, 2, 2)),
            dma((CHUNKS, 2, 2)),
            dma((CHUNKS, 2, 3, 2)),
            dma((CHUNKS, 2, 3, 2)),
            dma((n_w, 2, 3)),
            dma((n_w, 2, 3)),
            dma((parts, 2)),
            dma((parts, 2)),
            dma((parts, 2)),
            dma((parts, 2)),
            dma((sources,)),
            dma((sources,)),
            dma((parts,)),
            dma((parts,)),
        ],
        compiler_params=pltpu.CompilerParams(
            collective_id=0, has_side_effects=True, vmem_limit_bytes=VMEM_BYTES
        ),
        cost_estimate=pl.CostEstimate(
            flops=4 * tile * (keys + 2 * text) * width,
            bytes_accessed=12 * tile * width,
            transcendentals=heads * tile * (keys + 2 * text),
        ),
        name="joint_attention",
    )(
        text_length,
        image_query.reshape(tile, width),
        image_key.reshape(tile, width),
        image_value.reshape(tile, width),
        text_query,
        text_key,
        text_value,
    )
    return image_out.reshape(rows, cols, width), text_out


def solution(mesh):
    in_specs = (
        P(("batch", "height"), "width", None),
        P(("batch", "height"), "width", None),
        P(("batch", "height"), "width", None),
        P(("batch", "width"), None),
        P(("batch", "width"), None),
        P(("batch", "width"), None),
        P("batch"),
    )
    out_specs = (P(("batch", "height"), "width", None), P(("batch", "width"), None))
    return jax.shard_map(shards, mesh=mesh, in_specs=in_specs, out_specs=out_specs, check_vma=False)
```

```python
import functools
import math

import jax
import jax.numpy as jnp
from jax import lax
from jax.experimental import pallas as pl
from jax.experimental.pallas import tpu as pltpu
from jax.sharding import PartitionSpec as P

HEAD_DIM = 128
RADIUS = 8
CHUNKS = 4
MASKED = -1e30
VMEM_BYTES = 62 * 1024 * 1024
SCALE = math.log2(math.e) / math.sqrt(HEAD_DIM)
NT = (((1,), (1,)), ((), ()))


def dot_nt(a, b):
    return lax.dot_general(a, b, NT, preferred_element_type=jnp.float32)


def dot_nn(a, b):
    return jnp.dot(a, b, preferred_element_type=jnp.float32)


def dot_split(weight, value):
    high = weight.astype(jnp.bfloat16)
    low = (weight - high.astype(jnp.float32)).astype(jnp.bfloat16)
    return dot_nn(high, value) + dot_nn(low, value)


def joint(
    dims,
    length_ref,
    q_hbm,
    k_hbm,
    v_hbm,
    tq_hbm,
    tk_hbm,
    tv_hbm,
    image_out,
    text_out,
    q_ref,
    kbuf,
    vbuf,
    tk,
    tv,
    tq,
    xk,
    xv,
    obuf,
    rbuf,
    tout,
    bias,
    local_sem,
    zs,
    zr,
    vs,
    vr,
    ts,
    tr,
    ps,
    pr,
    xs,
    xr,
    os_,
    or_,
    fs,
    fr,
):
    n_h, n_w, rows, cols, heads, own_text, parts = dims
    tile = rows * cols
    strip = RADIUS * cols
    text = own_text * n_w
    groups = n_h // parts
    part_heads = heads // parts
    pc = part_heads * HEAD_DIM
    chunk_heads = heads // CHUNKS
    cc = chunk_heads * HEAD_DIM
    hc = cc // 2
    h = lax.axis_index("height")
    w = lax.axis_index("width")
    group = lax.div(h, parts)
    part = lax.rem(h, parts)
    par = lax.rem(h, 2)
    has_left, has_right = w > 0, w < n_w - 1
    has_up, has_down = h > 0, h < n_h - 1

    def at(hh, ww):
        return {"height": hh, "width": ww}

    def send(src, dst, s, r, device):
        return pltpu.make_async_remote_copy(
            src_ref=src,
            dst_ref=dst,
            send_sem=s,
            recv_sem=r,
            device_id=device,
            device_id_type=pl.DeviceIdType.MESH,
        )

    images = ((k_hbm, kbuf), (v_hbm, vbuf))
    texts = ((tk_hbm, tk), (tv_hbm, tv))
    part_cols = pl.ds(pl.multiple_of(part * pc, 128), pc)
    my_rows = pl.ds(pl.multiple_of(w * own_text, 16), own_text)

    barrier = pltpu.get_barrier_semaphore()
    greeted = 0
    for d in range(1, n_w):
        pl.semaphore_signal(barrier, inc=1, device_id=at(h, lax.rem(w + d, n_w)), device_id_type=pl.DeviceIdType.MESH)
        greeted += 1
    for d in range(1, n_h):
        pl.semaphore_signal(barrier, inc=1, device_id=at(lax.rem(h + d, n_h), w), device_id_type=pl.DeviceIdType.MESH)
        greeted += 1
    for g in range(1, groups):
        for d in range(1, n_w):
            pl.semaphore_signal(
                barrier,
                inc=1,
                device_id=at(lax.rem(h + g * parts, n_h), lax.rem(w + d, n_w)),
                device_id_type=pl.DeviceIdType.MESH,
            )
            greeted += 1
    pl.semaphore_wait(barrier, greeted)

    locals_ = []
    for i, (src, dst) in enumerate(images):
        locals_.append(pltpu.make_async_copy(src, dst.at[pl.ds(0, tile), :], local_sem.at[i]))
    my_slot = pl.ds(pl.multiple_of(part * tile, 16), tile)
    for i, (src, dst) in enumerate(((k_hbm, xk), (v_hbm, xv))):
        locals_.append(pltpu.make_async_copy(src.at[:, part_cols], dst.at[my_slot, :], local_sem.at[2 + i]))

    slabs = ((tq_hbm, tq, pl.ds(0, pc)), (tk_hbm, tk, part_cols), (tv_hbm, tv, part_cols))
    for i, (src, dst, columns) in enumerate(slabs):
        locals_.append(pltpu.make_async_copy(src.at[:, part_cols], dst.at[my_rows, columns], local_sem.at[4 + i]))
    locals_.append(pltpu.make_async_copy(q_hbm, q_ref, local_sem.at[7]))
    for copy in locals_:
        copy.start()

    def slab_sends(hop, way):
        owner = w - hop if way == 0 else w + hop
        owner_rows = pl.ds(pl.multiple_of(owner * own_text, 16), own_text)
        to = w + 1 if way == 0 else w - 1
        return [
            send(
                src.at[:, part_cols] if hop == 0 else dst.at[owner_rows, columns],
                dst.at[owner_rows, columns],
                ts.at[hop, way, i],
                tr.at[hop, way, i],
                at(h, to),
            )
            for i, (src, dst, columns) in enumerate(slabs)
        ]

    def slab_in(hop, way):
        return w > hop if way == 0 else w < n_w - 1 - hop

    def flipped(bit):
        return part + bit * (1 - 2 * lax.rem(lax.div(part, bit), 2))

    exchanges = []
    offsets = [0]
    bit = parts // 2
    while bit:
        stage = []
        for offset in offsets:
            held = part
            for b in range(8):
                if offset & (1 << b):
                    held = held + (1 << b) * (1 - 2 * lax.rem(lax.div(part, 1 << b), 2))
            columns = pl.ds(pl.multiple_of(held * pc, 128), pc)
            for i, (_, dst) in enumerate(texts):
                at_sem = len(offsets) + len(stage) // 2
                stage.append(
                    send(
                        dst.at[:, columns],
                        dst.at[:, columns],
                        ps.at[at_sem, i],
                        pr.at[at_sem, i],
                        at(group * parts + flipped(bit), w),
                    )
                )
        exchanges.append(stage)
        offsets = offsets + [o ^ bit for o in offsets]
        bit //= 2

    x_sends = []
    for d in range(1, parts):
        other = lax.rem(part + d, parts)
        other_cols = pl.ds(pl.multiple_of(other * pc, 128), pc)
        for i, (src, dst) in enumerate(((k_hbm, xk), (v_hbm, xv))):
            x_sends.append(
                send(src.at[:, other_cols], dst.at[my_slot, :], xs.at[d, i], xr.at[d, i], at(group * parts + other, w))
            )

    def side_sends(c, way):
        to = w + 1 if way == 0 else w - 1
        columns = pl.ds(c * cc, cc)
        return [
            send(
                src.at[:, columns],
                dst.at[pl.ds(tile * (1 + way), tile), columns],
                zs.at[c, way, i],
                zr.at[c, way, i],
                at(h, to),
            )
            for i, (src, dst) in enumerate(images)
        ]

    def strip_sends(c, way, piece):
        to = h + 1 if way == 0 else h - 1
        columns = pl.ds(c * cc, cc)
        start = tile - strip if way == 0 else 0
        slot = 3 * tile + (3 * way + piece) * strip
        return [
            send(
                (src if piece == 0 else dst).at[pl.ds(piece * tile + start, strip), columns],
                dst.at[pl.ds(slot, strip), columns],
                vs.at[c, way, piece, i],
                vr.at[c, way, piece, i],
                at(to, w),
            )
            for i, (src, dst) in enumerate(images)
        ]

    side_out = (has_right, has_left)
    side_in = (has_left, has_right)
    strip_out = (has_down, has_up)
    strip_in = (has_up, has_down)
    piece_there = (True, has_left, has_right)

    def start_chunk(c):
        for way in range(2):

            @pl.when(side_out[way])
            def _(way=way):
                for copy in side_sends(c, way):
                    copy.start()

            @pl.when(strip_out[way])
            def _(way=way):
                for copy in strip_sends(c, way, 0):
                    copy.start()

    def relay_chunk(c):
        for way in range(2):

            @pl.when(side_in[way])
            def _(way=way):
                for copy in side_sends(c, way):
                    copy.wait_recv()
                for up in range(2):

                    @pl.when(strip_out[up])
                    def _():
                        for copy in strip_sends(c, up, 1 + way):
                            copy.start()

    def wait_chunk(c):
        for way in range(2):
            for piece in range(3):

                @pl.when(strip_in[way] & piece_there[piece])
                def _(way=way, piece=piece):
                    for copy in strip_sends(c, way, piece):
                        copy.wait_recv()

    def finish_chunk(c):
        for way in range(2):

            @pl.when(side_out[way])
            def _(way=way):
                for copy in side_sends(c, way):
                    copy.wait_send()

            for piece in range(3):

                @pl.when(strip_out[way] & piece_there[piece])
                def _(way=way, piece=piece):
                    for copy in strip_sends(c, way, piece):
                        copy.wait_send()

    for way in range(2):

        @pl.when(side_out[way])
        def _(way=way):
            for copy in slab_sends(0, way):
                copy.start()

    for copy in x_sends:
        copy.start()
    start_chunk(0)

    def region(first, count, row_off, col_off, valid):
        key = lax.broadcasted_iota(jnp.int32, (tile, count), 1)
        query = lax.broadcasted_iota(jnp.int32, (tile, count), 0)
        delta_row = lax.div(key, cols) + row_off - lax.div(query, cols)
        delta_col = lax.rem(key, cols) + col_off - lax.rem(query, cols)
        near = delta_row * delta_row + delta_col * delta_col <= RADIUS * RADIUS
        limit = jnp.where(valid, 0.0, MASKED)
        bias[:, first : first + count] = jnp.where(near, limit, MASKED)

    region(0, tile, 0, 0, True)
    region(tile, tile, 0, -cols, has_left)
    region(2 * tile, tile, 0, cols, has_right)
    for way in range(2):
        row_off = -RADIUS if way == 0 else rows
        for piece in range(3):
            col_off = (0, -cols, cols)[piece]
            first = 3 * tile + (3 * way + piece) * strip
            region(first, strip, row_off, col_off, strip_in[way] & piece_there[piece])

            @pl.when(jnp.logical_not(strip_in[way] & piece_there[piece]))
            def _():
                for _, dst in images:
                    dst[first : first + strip, :] = jnp.zeros((strip, dst.shape[1]), dst.dtype)

        @pl.when(jnp.logical_not(side_in[way]))
        def _():
            for _, dst in images:
                first = tile * (1 + way)
                dst[first : first + tile, :] = jnp.zeros((tile, dst.shape[1]), dst.dtype)

    def text_bias():
        return jnp.where(lax.broadcasted_iota(jnp.int32, (1, text), 1) < length_ref[0], 0.0, MASKED)

    def attend_chunk(c):
        limit = text_bias()

        def one_head(j, carry):
            column = pl.ds(pl.multiple_of(c * cc + j * HEAD_DIM, 128), HEAD_DIM)
            query = q_ref[:, column]
            score_win = dot_nt(query, kbuf[:, column]) + bias[...]
            score_text = dot_nt(query, tk[:, column]) + limit
            peak = jnp.maximum(
                jnp.max(score_win, axis=1, keepdims=True), jnp.max(score_text, axis=1, keepdims=True)
            )
            weight_win = jnp.exp2((score_win - peak) * SCALE)
            weight_text = jnp.exp2((score_text - peak) * SCALE)
            total = jnp.sum(weight_win, axis=1, keepdims=True) + jnp.sum(weight_text, axis=1, keepdims=True)
            numer = dot_nn(weight_win.astype(jnp.bfloat16), vbuf[:, column])
            numer = numer + dot_nn(weight_text.astype(jnp.bfloat16), tv[:, column])
            image_out[:, column] = (numer / total).astype(jnp.bfloat16)
            return carry

        lax.fori_loop(0, chunk_heads, one_head, 0, unroll=2)

    block = math.gcd(text, 128)

    def text_partial(b, carry):
        block_rows = pl.ds(pl.multiple_of(b * block, block), block)
        lane = lax.broadcasted_iota(jnp.int32, (block, 128), 1)
        stats = jnp.zeros((block, 128), jnp.float32)
        for j in range(part_heads):
            column = slice(j * HEAD_DIM, (j + 1) * HEAD_DIM)
            score = dot_nt(tq[block_rows, column], xk[:, column])
            peak = jnp.max(score, axis=1, keepdims=True)
            weight = jnp.exp2((score - peak) * SCALE)
            total = jnp.sum(weight, axis=1, keepdims=True)
            numer = dot_split(weight, xv[:, column])
            obuf[block_rows, column] = (numer / total).astype(jnp.bfloat16)
            log_total = peak * SCALE + jnp.log2(total)
            for third in range(3):
                piece = log_total.astype(jnp.bfloat16).astype(jnp.float32)
                stats = jnp.where(lane == 32 * third + j, piece, stats)
                log_total = log_total - piece
        obuf[block_rows, pc : pc + 128] = stats.astype(jnp.bfloat16)
        return carry

    o_sends = []
    for g in range(groups):
        for d in range(n_w):
            if g or d:
                to_w = lax.rem(w + d, n_w)
                their_rows = pl.ds(pl.multiple_of(to_w * own_text, 16), own_text)
                at_slot = g * n_w + d
                o_sends.append(
                    send(
                        obuf.at[their_rows, :],
                        rbuf.at[at_slot],
                        os_.at[at_slot],
                        or_.at[at_slot],
                        at(lax.rem(h + g * parts, n_h), to_w),
                    )
                )

    f_sends = [
        send(
            tout.at[:, part_cols],
            tout.at[:, part_cols],
            fs.at[d],
            fr.at[d],
            at(group * parts + lax.rem(part + d, parts), w),
        )
        for d in range(1, parts)
    ]

    def text_combine():
        limit = text_bias()
        for j in range(part_heads):
            column = slice(j * HEAD_DIM, (j + 1) * HEAD_DIM)
            wide = pl.ds(pl.multiple_of(part * pc + j * HEAD_DIM, 128), HEAD_DIM)
            score = dot_nt(tq[my_rows, column], tk[:, wide]) + limit
            pieces = [(obuf[my_rows, column], obuf[my_rows, pc : pc + 128])]
            for s in range(1, groups * n_w):
                pieces.append((rbuf[s, :, column], rbuf[s, :, pc : pc + 128]))
            logs = []
            for _, stats in pieces:
                stats = stats.astype(jnp.float32)
                logs.append(stats[:, j : j + 1] + stats[:, 32 + j : 33 + j] + stats[:, 64 + j : 65 + j])
            peak = jnp.max(score, axis=1, keepdims=True) * SCALE
            for log_total in logs:
                peak = jnp.maximum(peak, log_total)
            weight = jnp.exp2(score * SCALE - peak)
            total = jnp.sum(weight, axis=1, keepdims=True)
            numer = dot_split(weight, tv[:, wide])
            for (value, _), log_total in zip(pieces, logs):
                factor = jnp.exp2(log_total - peak)
                total = total + factor
                numer = numer + factor * value.astype(jnp.float32)
            tout[:, wide] = (numer / total).astype(jnp.bfloat16)

    for copy in locals_:
        copy.wait()
    for hop in range(n_w - 1):
        for way in range(2):

            @pl.when(slab_in(hop, way))
            def _(way=way, hop=hop):
                for copy in slab_sends(hop, way):
                    copy.wait_recv()

            if hop + 1 < n_w - 1:

                @pl.when(slab_in(hop, way) & side_out[way])
                def _(way=way, hop=hop):
                    for copy in slab_sends(hop + 1, way):
                        copy.start()

        if hop + 1 < CHUNKS:
            start_chunk(hop + 1)
    for c in range(n_w, CHUNKS):
        start_chunk(c)

    def run_exchange(k):
        if k > 0:
            for copy in exchanges[k - 1]:
                copy.wait_recv()
        if k < len(exchanges):
            for copy in exchanges[k]:
                copy.start()

    run_exchange(0)
    relay_chunk(0)
    for copy in x_sends:
        copy.wait_recv()
    lax.fori_loop(0, text // block, text_partial, 0)
    for copy in o_sends:
        copy.start()
    run_exchange(1)
    relay_chunk(1)
    for k in range(2, len(exchanges) + 1):
        run_exchange(k)
    wait_chunk(0)
    attend_chunk(0)
    relay_chunk(2)
    wait_chunk(1)
    attend_chunk(1)
    relay_chunk(3)
    for copy in o_sends:
        copy.wait_recv()
    text_combine()
    for copy in f_sends:
        copy.start()
    wait_chunk(2)
    attend_chunk(2)
    wait_chunk(3)
    attend_chunk(3)
    for copy in f_sends:
        copy.wait_recv()
    text_out[...] = tout[...]
    for stage in exchanges:
        for copy in stage:
            copy.wait_send()
    for copy in x_sends + o_sends + f_sends:
        copy.wait_send()
    for way in range(2):

        @pl.when(side_out[way])
        def _(way=way):
            for copy in slab_sends(0, way):
                copy.wait_send()

        for hop in range(1, n_w - 1):

            @pl.when(slab_in(hop - 1, way) & side_out[way])
            def _(way=way, hop=hop):
                for copy in slab_sends(hop, way):
                    copy.wait_send()

    for c in range(CHUNKS):
        finish_chunk(c)


def shards(image_query, image_key, image_value, text_query, text_key, text_value, text_length):
    rows, cols, width = image_query.shape
    heads = width // HEAD_DIM
    n_h, n_w = lax.axis_size("height"), lax.axis_size("width")
    own_text = text_query.shape[0]
    parts = math.gcd(math.gcd(heads, n_h), 8)
    tile = rows * cols
    strip = RADIUS * cols
    text = own_text * n_w
    sources = (n_h // parts) * n_w
    pc = width // parts
    keys = 3 * tile + 6 * strip
    bf16, f32 = jnp.bfloat16, jnp.float32
    dma = pltpu.SemaphoreType.DMA
    any_spec = pl.BlockSpec(memory_space=pl.ANY)
    vmem_spec = pl.BlockSpec(memory_space=pltpu.VMEM)
    image_out, text_out = pl.pallas_call(
        functools.partial(joint, (n_h, n_w, rows, cols, heads, own_text, parts)),
        out_shape=(
            jax.ShapeDtypeStruct((tile, width), bf16),
            jax.ShapeDtypeStruct((own_text, width), bf16),
        ),
        in_specs=[pl.BlockSpec(memory_space=pltpu.SMEM)] + [any_spec] * 6,
        out_specs=(vmem_spec, vmem_spec),
        scratch_shapes=[
            pltpu.VMEM((tile, width), bf16),
            pltpu.VMEM((keys, width), bf16),
            pltpu.VMEM((keys, width), bf16),
            pltpu.VMEM((text, width), bf16),
            pltpu.VMEM((text, width), bf16),
            pltpu.VMEM((text, pc), bf16),
            pltpu.VMEM((parts * tile, pc), bf16),
            pltpu.VMEM((parts * tile, pc), bf16),
            pltpu.VMEM((text, pc + 128), bf16),
            pltpu.VMEM((sources, own_text, pc + 128), bf16),
            pltpu.VMEM((own_text, width), bf16),
            pltpu.VMEM((tile, keys), f32),
            dma((8,)),
            dma((CHUNKS, 2, 2)),
            dma((CHUNKS, 2, 2)),
            dma((CHUNKS, 2, 3, 2)),
            dma((CHUNKS, 2, 3, 2)),
            dma((n_w, 2, 3)),
            dma((n_w, 2, 3)),
            dma((parts, 2)),
            dma((parts, 2)),
            dma((parts, 2)),
            dma((parts, 2)),
            dma((sources,)),
            dma((sources,)),
            dma((parts,)),
            dma((parts,)),
        ],
        compiler_params=pltpu.CompilerParams(
            collective_id=0, has_side_effects=True, vmem_limit_bytes=VMEM_BYTES
        ),
        cost_estimate=pl.CostEstimate(
            flops=4 * tile * (keys + 2 * text) * width,
            bytes_accessed=12 * tile * width,
            transcendentals=heads * tile * (keys + 2 * text),
        ),
        name="joint_attention",
    )(
        text_length,
        image_query.reshape(tile, width),
        image_key.reshape(tile, width),
        image_value.reshape(tile, width),
        text_query,
        text_key,
        text_value,
    )
    return image_out.reshape(rows, cols, width), text_out


def solution(mesh):
    in_specs = (
        P(("batch", "height"), "width", None),
        P(("batch", "height"), "width", None),
        P(("batch", "height"), "width", None),
        P(("batch", "width"), None),
        P(("batch", "width"), None),
        P(("batch", "width"), None),
        P("batch"),
    )
    out_specs = (P(("batch", "height"), "width", None), P(("batch", "width"), None))
    return jax.shard_map(shards, mesh=mesh, in_specs=in_specs, out_specs=out_specs, check_vma=False)
```
